32 devices in a mesh: section: 4 (over y, core), tensor: 4 (over z), dp: 2 (over x).
Axes of the slice: x: 2, y: 2, z: 4, core: 2. Of those that a mesh axis runs over, the one named last changes fastest.
Arguments:
- hidden: bfloat16 [64, 8192], P(('section', 'dp'), 'tensor'), may hold values from -250 to 250
- vocab_weight: bfloat16 [8192, 10240], P(None, ('section', 'tensor')), may hold values from -0.6 to 0.6
- target_ids: int32 [64], P(('section', 'dp')), may hold values from 0 to 10239
- ref_logp: float32 [64], P(('section', 'dp')), may hold values from -8 to -0.5
- response_lengths: int32 [8], P(('section', 'dp')), may hold values from 1 to 8
Outputs:
- token_logp: float32 [64], P(('section', 'dp'))
- entropy: float32 [64], P(('section', 'dp'))
- kl_term: float32 [64], P(('section', 'dp'))
The draws below stay inside these ranges and needn't reach their ends.
All inputs are finite; a program needn't handle non-finite values.
Results may differ from the reference program's by a relative error of at most 0.0015.
Values may be sent and summed in bfloat16 or wider, within the bound.
A program may use at most 64 MiB of HBM per device.

```python
import math
import jax
import jax.numpy as jnp
import numpy as np
from jax import lax

D = 8192
VOC_DEV = 640
VOCAB = 10240
TOKENS = 64
SPAN = 8
SEQS = 8


def feature_mean(key):
    return jnp.clip(0.1 * jax.random.normal(jax.random.fold_in(key, 99), (D,), jnp.float32), -0.4, 0.4)


def draw_vocab_weight(key, part):
    noise = jnp.clip(0.033 * jax.random.normal(jax.random.fold_in(key, 31), (D, VOCAB), jnp.float32), -0.2, 0.2)
    return (noise + feature_mean(key)[:, None]).astype(jnp.bfloat16)


def draw_hidden(key, part):
    first = jax.random.fold_in(jax.random.fold_in(key, 17), 0)
    values = jax.random.normal(first, (TOKENS, D), jnp.float32)
    values = jnp.clip(values, -6.0, 6.0)
    mean = feature_mean(key)
    direction = mean / jnp.sum(mean * mean)
    chosen = jax.random.bernoulli(jax.random.fold_in(key, 41), 0.25, (TOKENS, 1)).astype(jnp.float32)
    shift = jax.random.uniform(jax.random.fold_in(key, 43), (TOKENS, 1), jnp.float32, 220.0, 450.0)
    values = jnp.clip(values + chosen * shift * direction[None, :], -250.0, 250.0)
    return values.astype(jnp.bfloat16)


def plant(entries, own_key, low, largest):
    shape = entries.shape
    index_at = [jax.random.randint(jax.random.fold_in(own_key, axis), (), 0, shape[axis]) for axis in range(len(shape))]
    entries = entries.at[tuple(index_at)].set(low)
    longest = shape.index(max(shape))
    index_at[longest] = (index_at[longest] + 1) % shape[longest]
    return entries.at[tuple(index_at)].set(largest)


def levels(own_key, shape, pieces, smallest, top_value):
    def one(axis_at, parts):
        steps = jax.random.uniform(jax.random.fold_in(jax.random.fold_in(own_key, 6), axis_at), (parts,), jnp.float32, smallest / len(pieces), top_value / len(pieces))
        return jnp.repeat(jnp.exp(steps), shape[axis_at] // parts).reshape((-1,) + (1,) * (len(shape) - axis_at - 1))

    gain = one(*pieces[0])
    for cut in pieces[1:]:
        gain = gain * one(*cut)
    return gain


def rank_bounds(number_of, lean):
    portions = [(1 << 20) // math.isqrt(standing ** lean) + 1 for standing in range(1, number_of + 1)]
    spread = 1 + sum(portions) // (1 << 30)
    return np.cumsum(np.array([max(1, weight // spread) for weight in portions]))


def skewed_ids(rng, extent, number_of, slope):
    listing = rank_bounds(number_of, slope)
    ticket = jax.random.randint(jax.random.fold_in(rng, 1), extent, 0, int(listing[number_of - 1]))
    standing = jnp.searchsorted(jnp.asarray(listing, jnp.int32), ticket, side="right")
    return jax.random.permutation(jax.random.fold_in(rng, 2), number_of)[standing].astype(jnp.int32)


def setup_inputs(seed: int = 0) -> dict:
    key_list = jax.random.split(jax.random.key(seed), 6)
    return {
        "hidden": draw_hidden(jax.random.fold_in(key_list[5], 71), 0),
        "vocab_weight": draw_vocab_weight(jax.random.fold_in(key_list[5], 71), 0),
        "target_ids": plant(skewed_ids(key_list[2], (TOKENS,), VOCAB, 2), jax.random.fold_in(key_list[2], 3), 0, VOCAB - 1).astype(jnp.int32),
        "ref_logp": jnp.clip(-8.0 + 7.5 * jax.random.uniform(key_list[3], (TOKENS,), jnp.float32) ** levels(key_list[3], (TOKENS,), ((0, 8),), -0.2, 0.2), -8.0, -0.5),
        "response_lengths": plant(jax.random.randint(key_list[4], (SEQS,), 1, SPAN + 1), jax.random.fold_in(key_list[4], 1), 1, SPAN).astype(jnp.int32),
    }


def block_stats(hidden_f, vocab_weight, target_ids, index):
    start = index * VOC_DEV
    cols = lax.dynamic_slice_in_dim(vocab_weight, start, VOC_DEV, 1).astype(jnp.float32)
    logits = jnp.dot(hidden_f, cols, preferred_element_type=jnp.float32)
    top = jnp.max(logits, axis=1)
    expo = jnp.exp(logits - top[:, None])
    total = jnp.sum(expo, axis=1)
    moment = jnp.sum(expo * logits, axis=1)
    column = start + jnp.arange(VOC_DEV, dtype=jnp.int32)
    picked = jnp.sum(jnp.where(target_ids[:, None] == column[None, :], logits, 0.0), axis=1)
    return top, total, moment, picked


def reference(hidden, vocab_weight, target_ids, ref_logp, response_lengths):
    hidden_f = hidden.astype(jnp.float32)
    count = VOCAB // VOC_DEV
    tops, totals, moments, pickeds = lax.map(lambda k: block_stats(hidden_f, vocab_weight, target_ids, k), jnp.arange(count, dtype=jnp.int32))
    top = jnp.max(tops, axis=0)
    scale = jnp.exp(tops - top[None, :])
    total = jnp.sum(totals * scale, axis=0)
    moment = jnp.sum(moments * scale, axis=0)
    picked = jnp.sum(pickeds, axis=0)
    lse = top + jnp.log(total)
    logp = picked - lse
    ent = lse - moment / total
    token = jnp.arange(TOKENS, dtype=jnp.int32)
    owner = token // SPAN
    slot = token % SPAN
    live = (slot < response_lengths[owner]).astype(jnp.float32)
    return logp * live, ent * live, (logp - ref_logp) * live
```

```python
import functools

import jax
import jax.numpy as jnp
from jax import lax
from jax.experimental import pallas as pl
from jax.experimental.pallas import tpu as pltpu
from jax.sharding import PartitionSpec as P

MESH = pl.DeviceIdType.MESH
LANES = 128


def repeat(count, body):
    if count <= 16:
        for i in range(count):
            body(i)
    else:
        lax.fori_loop(0, count, lambda i, _: (body(i), 0)[1], 0)


def kernel(
    sections, tensors, hidden, weight, ids, ref_logp, lengths,
    out_logp, out_ent, out_kl,
    w, g, id_rows, ref_v, len_v, stat, merged,
    w_sem, own_sem, block_recv, a_send, b_send, c_send, id_send, id_recv, s_send, s_recv,
):
    rows, width = hidden.shape
    voc_dev = weight.shape[1]
    pairs = sections // 2
    peers = sections * tensors
    group = LANES // (4 * rows)
    section = lax.axis_index("section")
    tensor = lax.axis_index("tensor")
    core = section % 2
    pair = section // 2
    sibling = section + 1 - 2 * core
    me = section * tensors + tensor

    def nth(j):
        if tensors & (tensors - 1):
            return (tensor + j) % tensors, (tensor + tensors - j) % tensors
        at, bit = tensor, 1
        while bit < tensors:
            if j & bit:
                at = at + bit - 2 * bit * ((tensor // bit) % 2)
            bit *= 2
        return at, at

    loads = []
    for j in range(tensors):
        _, source = nth(j)
        begin = pl.multiple_of(source * width, width)
        loads.append(pltpu.make_async_copy(weight.at[pl.ds(begin, width)], w.at[j], w_sem.at[j]))
        loads[-1].start()
    own = pltpu.make_async_copy(hidden, g.at[tensor, section], own_sem.at[0])
    own_id = pltpu.make_async_copy(ids, id_rows.at[section], own_sem.at[1])
    own_ref = pltpu.make_async_copy(ref_logp, ref_v, own_sem.at[2])
    own_len = pltpu.make_async_copy(lengths, len_v, own_sem.at[3])
    for copy in (own, own_id, own_ref, own_len):
        copy.start()

    barrier = pltpu.get_barrier_semaphore()

    def greet(k):
        other = (me + k + 1) % peers
        pl.semaphore_signal(
            barrier, inc=1, device_id={"section": other // tensors, "tensor": other % tensors},
            device_id_type=MESH,
        )

    repeat(peers - 1, greet)
    pl.semaphore_wait(barrier, peers - 1)

    def block(source, t, s, send, to_section, to_tensor):
        return pltpu.make_async_remote_copy(
            src_ref=source, dst_ref=g.at[t, s], send_sem=send, recv_sem=block_recv.at[t, s],
            device_id={"section": to_section, "tensor": to_tensor}, device_id_type=MESH,
        )

    def copy_a(j):
        return block(hidden, tensor, section, a_send.at[j], section, nth(j)[0])

    def copy_b(j, source, k):
        to = ((pair + k + 1) % pairs) * 2 + core
        return block(source, nth(j)[1], section, b_send.at[j, k], to, tensor)

    def copy_c(j, source, k):
        s = ((pair + k) % pairs) * 2 + core
        return block(source, nth(j)[1], s, c_send.at[j, k], sibling, tensor)

    def arrived(t, s):
        pltpu.make_async_copy(g.at[t, s], g.at[t, s], block_recv.at[t, s]).wait()

    def id_copy(k):
        return pltpu.make_async_remote_copy(
            src_ref=ids, dst_ref=id_rows.at[section], send_sem=id_send.at[k],
            recv_sem=id_recv.at[section],
            device_id={"section": (section + k + 1) % sections}, device_id_type=MESH,
        )

    for j in range(1, tensors):
        copy_a(j).start()
    repeat(pairs - 1, lambda k: copy_b(0, hidden, k).start())
    copy_c(0, hidden, 0).start()
    repeat(sections - 1, lambda k: id_copy(k).start())

    acc = None
    own.wait()

    def forward_own(j):
        t = nth(j)[1]
        arrived(t, section)
        repeat(pairs - 1, lambda k: copy_b(j, g.at[t, section], k).start())
        copy_c(j, g.at[t, section], 0).start()

    def forward_pairs(j):
        t = nth(j)[1]

        def one(k):
            s = ((pair + k + 1) % pairs) * 2 + core
            arrived(t, s)
            copy_c(j, g.at[t, s], k + 1).start()

        repeat(pairs - 1, one)

    def product(j):
        t = nth(j)[1]
        repeat(pairs, lambda k: arrived(t, ((pair + k) % pairs) * 2 + 1 - core))
        loads[j].wait()
        x = g[t].astype(jnp.float32).reshape(sections * rows, width).astype(jnp.bfloat16)
        return jnp.dot(x, w[j], preferred_element_type=jnp.float32)

    forward_pairs(0)
    for j in range(1, tensors):
        forward_own(j)
        forward_pairs(j)
        part = product(j - 1)
        acc = part if acc is None else acc + part
    part = product(tensors - 1)
    logits = part if acc is None else acc + part

    own_id.wait()

    def id_wait(k):
        s = (section + k + 1) % sections
        pltpu.make_async_copy(id_rows.at[s], id_rows.at[s], id_recv.at[s]).wait()

    repeat(sections - 1, id_wait)
    eye = lax.broadcasted_iota(jnp.int32, (rows, rows), 0) == lax.broadcasted_iota(
        jnp.int32, (rows, rows), 1
    )
    columns = []
    for s in range(sections):
        row = jnp.broadcast_to(id_rows[s].astype(jnp.float32), (rows, rows))
        columns.append(jnp.sum(jnp.where(eye, row, 0.0), axis=1, keepdims=True))
    column = jnp.concatenate(columns, axis=0).astype(jnp.int32) - me * voc_dev

    top = jnp.max(logits, axis=1, keepdims=True)
    expo = jnp.exp(logits - top)
    total = jnp.sum(expo, axis=1, keepdims=True)
    moment = jnp.sum(expo * logits, axis=1, keepdims=True)
    at = lax.broadcasted_iota(jnp.int32, logits.shape, 1)
    picked = jnp.sum(jnp.where(at == column, logits, 0.0), axis=1, keepdims=True)

    span = group * rows
    diagonal = lax.broadcasted_iota(jnp.int32, (LANES, LANES), 0) == lax.broadcasted_iota(
        jnp.int32, (LANES, LANES), 1
    )
    for c in range(sections // group):
        piece = jnp.concatenate(
            [item[c * span : (c + 1) * span] for item in (top, total, moment, picked)], axis=0
        )
        stat[c] = jnp.sum(
            jnp.where(diagonal, jnp.broadcast_to(piece, (LANES, LANES)), 0.0), axis=0, keepdims=True
        )

    def stat_copy(k):
        other = (me + k + 1) % peers
        to = other // tensors
        return pltpu.make_async_remote_copy(
            src_ref=stat.at[to // group], dst_ref=merged.at[me], send_sem=s_send.at[k],
            recv_sem=s_recv.at[me],
            device_id={"section": to, "tensor": other % tensors}, device_id_type=MESH,
        )

    repeat(peers - 1, lambda k: stat_copy(k).start())
    merged[me] = stat[section // group]

    for j in range(1, tensors):
        copy_a(j).wait_send()
    for j in range(tensors):
        repeat(pairs - 1, lambda k: copy_b(j, hidden, k).wait_send())
        repeat(pairs, lambda k: copy_c(j, hidden, k).wait_send())
    repeat(sections - 1, lambda k: id_copy(k).wait_send())
    own_ref.wait()
    own_len.wait()

    def stat_wait(k):
        other = (me + k + 1) % peers
        pltpu.make_async_copy(merged.at[other], merged.at[other], s_recv.at[other]).wait()

    repeat(peers - 1, stat_wait)
    every = merged[...].reshape(peers, LANES)
    lane = lax.broadcasted_iota(jnp.int32, (1, LANES), 1)
    best = jnp.max(every, axis=0, keepdims=True)
    scale = jnp.exp(every - best)
    factor = jnp.where(
        lane < 2 * span, pltpu.roll(scale, span, 1),
        jnp.where(lane < 3 * span, pltpu.roll(scale, 2 * span, 1), 1.0),
    )
    result = jnp.where(lane < span, best, jnp.sum(every * factor, axis=0, keepdims=True))
    mine = result
    for k in range(1, group):
        mine = jnp.where(section % group == k, pltpu.roll(result, LANES - k * rows, 1), mine)
    top = mine
    total = pltpu.roll(mine, LANES - span, 1)
    moment = pltpu.roll(mine, LANES - 2 * span, 1)
    picked = pltpu.roll(mine, LANES - 3 * span, 1)
    top, total, moment, picked = [item[:, :rows] for item in (top, total, moment, picked)]
    lse = top + jnp.log(total)
    logp = picked - lse
    ent = lse - moment / total
    live = (lane[:, :rows] < len_v[...]).astype(jnp.float32)
    out_logp[...] = logp * live
    out_ent[...] = ent * live
    out_kl[...] = (logp - ref_v[...]) * live
    repeat(peers - 1, lambda k: stat_copy(k).wait_send())


def per_device(sections, tensors, hidden, weight, ids, ref_logp, lengths):
    rows, width = hidden.shape
    depth, voc_dev = weight.shape
    pairs = sections // 2
    peers = sections * tensors
    chunks = sections * rows * 4 // LANES
    anywhere = pl.BlockSpec(memory_space=pl.ANY)
    dma = pltpu.SemaphoreType.DMA
    outs = pl.pallas_call(
        functools.partial(kernel, sections, tensors),
        out_shape=[jax.ShapeDtypeStruct((1, rows), jnp.float32)] * 3,
        in_specs=[anywhere] * 5,
        out_specs=[pl.BlockSpec(memory_space=pltpu.VMEM)] * 3,
        scratch_shapes=[
            pltpu.VMEM((tensors, width, voc_dev), jnp.bfloat16),
            pltpu.VMEM((tensors, sections, rows, width), jnp.bfloat16),
            pltpu.VMEM((sections, 1, rows), jnp.int32),
            pltpu.VMEM((1, rows), jnp.float32),
            pltpu.VMEM((1, 1), jnp.int32),
            pltpu.VMEM((chunks, 1, LANES), jnp.float32),
            pltpu.VMEM((peers, 1, LANES), jnp.float32),
            dma((tensors,)),
            dma((4,)),
            dma((tensors, sections)),
            dma((tensors,)),
            dma((tensors, pairs)),
            dma((tensors, pairs)),
            dma((sections,)),
            dma((sections,)),
            dma((peers,)),
            dma((peers,)),
        ],
        compiler_params=pltpu.CompilerParams(
            collective_id=0, has_side_effects=True, vmem_limit_bytes=48 * 1024 * 1024
        ),
    )(hidden, weight, ids.reshape(1, rows), ref_logp.reshape(1, rows), lengths.reshape(1, 1))
    return tuple(item.reshape(rows) for item in outs)


def solution(mesh):
    in_specs = (
        P(("section", "dp"), "tensor"),
        P(None, ("section", "tensor")),
        P(("section", "dp")),
        P(("section", "dp")),
        P(("section", "dp")),
    )
    out_specs = (P(("section", "dp")), P(("section", "dp")), P(("section", "dp")))
    return jax.shard_map(
        functools.partial(per_device, mesh.shape["section"], mesh.shape["tensor"]),
        mesh=mesh, in_specs=in_specs, out_specs=out_specs, check_vma=False,
    )
```

```python
import functools

import jax
import jax.numpy as jnp
from jax import lax
from jax.experimental import pallas as pl
from jax.experimental.pallas import tpu as pltpu
from jax.sharding import PartitionSpec as P

MESH = pl.DeviceIdType.MESH
LANES = 128
DIRECT = ()


def repeat(count, body):
    if count <= 16:
        for i in range(count):
            body(i)
    else:
        lax.fori_loop(0, count, lambda i, _: (body(i), 0)[1], 0)


def kernel(
    sections, tensors, hidden, weight, ids, ref_logp, lengths,
    out_logp, out_ent, out_kl,
    w, g, id_rows, ref_v, len_v, stat, merged,
    w_sem, own_sem, block_recv, a_send, b_send, c_send, id_send, id_recv, s_send, s_recv,
):
    rows, width = hidden.shape
    voc_dev = weight.shape[1]
    pairs = sections // 2
    peers = sections * tensors
    group = LANES // (4 * rows)
    section = lax.axis_index("section")
    tensor = lax.axis_index("tensor")
    core = section % 2
    pair = section // 2
    sibling = section + 1 - 2 * core
    me = section * tensors + tensor

    def nth(j):
        if tensors & (tensors - 1):
            return (tensor + j) % tensors, (tensor + tensors - j) % tensors
        at, bit = tensor, 1
        while bit < tensors:
            if j & bit:
                at = at + bit - 2 * bit * ((tensor // bit) % 2)
            bit *= 2
        return at, at

    loads = []
    for j in range(tensors):
        _, source = nth(j)
        begin = pl.multiple_of(source * width, width)
        loads.append(pltpu.make_async_copy(weight.at[pl.ds(begin, width)], w.at[j], w_sem.at[j]))
        loads[-1].start()
    own = pltpu.make_async_copy(hidden, g.at[tensor, section], own_sem.at[0])
    own_id = pltpu.make_async_copy(ids, id_rows.at[section], own_sem.at[1])
    own_ref = pltpu.make_async_copy(ref_logp, ref_v, own_sem.at[2])
    own_len = pltpu.make_async_copy(lengths, len_v, own_sem.at[3])
    for copy in (own, own_id, own_ref, own_len):
        copy.start()

    barrier = pltpu.get_barrier_semaphore()

    def greet(k):
        other = (me + k + 1) % peers
        pl.semaphore_signal(
            barrier, inc=1, device_id={"section": other // tensors, "tensor": other % tensors},
            device_id_type=MESH,
        )

    repeat(peers - 1, greet)
    pl.semaphore_wait(barrier, peers - 1)

    def block(source, t, s, send, to_section, to_tensor):
        return pltpu.make_async_remote_copy(
            src_ref=source, dst_ref=g.at[t, s], send_sem=send, recv_sem=block_recv.at[t, s],
            device_id={"section": to_section, "tensor": to_tensor}, device_id_type=MESH,
        )

    def copy_a(j):
        return block(hidden, tensor, section, a_send.at[j], section, nth(j)[0])

    def copy_b(j, source, k):
        to = ((pair + k + 1) % pairs) * 2 + core
        t, to_tensor = (tensor, nth(j)[0]) if j in DIRECT else (nth(j)[1], tensor)
        return block(source, t, section, b_send.at[j, k], to, to_tensor)

    def copy_c(j, source, k):
        s = ((pair + k) % pairs) * 2 + core
        return block(source, nth(j)[1], s, c_send.at[j, k], sibling, tensor)

    def arrived(t, s):
        pltpu.make_async_copy(g.at[t, s], g.at[t, s], block_recv.at[t, s]).wait()

    def id_copy(k):
        return pltpu.make_async_remote_copy(
            src_ref=ids, dst_ref=id_rows.at[section], send_sem=id_send.at[k],
            recv_sem=id_recv.at[section],
            device_id={"section": (section + k + 1) % sections}, device_id_type=MESH,
        )

    repeat(pairs - 1, lambda k: copy_b(0, hidden, k).start())
    for j in range(1, tensors):
        copy_a(j).start()
    for j in DIRECT:
        repeat(pairs - 1, lambda k: copy_b(j, hidden, k).start())
    copy_c(0, hidden, 0).start()
    repeat(sections - 1, lambda k: id_copy(k).start())

    acc = None
    own.wait()

    def forward_own(j):
        t = nth(j)[1]
        arrived(t, section)
        if j not in DIRECT:
            repeat(pairs - 1, lambda k: copy_b(j, g.at[t, section], k).start())
        copy_c(j, g.at[t, section], 0).start()

    def forward_pairs(j):
        t = nth(j)[1]

        def one(k):
            s = ((pair + k + 1) % pairs) * 2 + core
            arrived(t, s)
            copy_c(j, g.at[t, s], k + 1).start()

        repeat(pairs - 1, one)

    def product(j):
        t = nth(j)[1]
        repeat(pairs, lambda k: arrived(t, ((pair + k) % pairs) * 2 + 1 - core))
        loads[j].wait()
        x = g[t].astype(jnp.float32).reshape(sections * rows, width).astype(jnp.bfloat16)
        return jnp.dot(x, w[j], preferred_element_type=jnp.float32)

    forward_own(1)
    forward_pairs(0)
    for j in range(2, tensors):
        forward_own(j)
    for j in range(1, tensors):
        forward_pairs(j)
        part = product(j - 1)
        acc = part if acc is None else acc + part
    logits = acc + product(tensors - 1)

    own_id.wait()

    def id_wait(k):
        s = (section + k + 1) % sections
        pltpu.make_async_copy(id_rows.at[s], id_rows.at[s], id_recv.at[s]).wait()

    repeat(sections - 1, id_wait)
    eye = lax.broadcasted_iota(jnp.int32, (rows, rows), 0) == lax.broadcasted_iota(
        jnp.int32, (rows, rows), 1
    )
    columns = []
    for s in range(sections):
        row = jnp.broadcast_to(id_rows[s].astype(jnp.float32), (rows, rows))
        columns.append(jnp.sum(jnp.where(eye, row, 0.0), axis=1, keepdims=True))
    column = jnp.concatenate(columns, axis=0).astype(jnp.int32) - me * voc_dev

    top = jnp.max(logits, axis=1, keepdims=True)
    expo = jnp.exp(logits - top)
    total = jnp.sum(expo, axis=1, keepdims=True)
    moment = jnp.sum(expo * logits, axis=1, keepdims=True)
    at = lax.broadcasted_iota(jnp.int32, logits.shape, 1)
    picked = jnp.sum(jnp.where(at == column, logits, 0.0), axis=1, keepdims=True)

    span = group * rows
    diagonal = lax.broadcasted_iota(jnp.int32, (LANES, LANES), 0) == lax.broadcasted_iota(
        jnp.int32, (LANES, LANES), 1
    )
    for c in range(sections // group):
        piece = jnp.concatenate(
            [item[c * span : (c + 1) * span] for item in (top, total, moment, picked)], axis=0
        )
        stat[c] = jnp.sum(
            jnp.where(diagonal, jnp.broadcast_to(piece, (LANES, LANES)), 0.0), axis=0, keepdims=True
        )

    def stat_copy(k):
        other = (me + k + 1) % peers
        to = other // tensors
        return pltpu.make_async_remote_copy(
            src_ref=stat.at[to // group], dst_ref=merged.at[me], send_sem=s_send.at[k],
            recv_sem=s_recv.at[me],
            device_id={"section": to, "tensor": other % tensors}, device_id_type=MESH,
        )

    repeat(peers - 1, lambda k: stat_copy(k).start())
    merged[me] = stat[section // group]

    for j in range(1, tensors):
        copy_a(j).wait_send()
    for j in range(tensors):
        repeat(pairs - 1, lambda k: copy_b(j, hidden, k).wait_send())
        repeat(pairs, lambda k: copy_c(j, hidden, k).wait_send())
    repeat(sections - 1, lambda k: id_copy(k).wait_send())
    own_ref.wait()
    own_len.wait()

    def stat_wait(k):
        other = (me + k + 1) % peers
        pltpu.make_async_copy(merged.at[other], merged.at[other], s_recv.at[other]).wait()

    repeat(peers - 1, stat_wait)
    every = merged[...].reshape(peers, LANES)
    lane = lax.broadcasted_iota(jnp.int32, (1, LANES), 1)
    best = jnp.max(every, axis=0, keepdims=True)
    scale = jnp.exp(every - best)
    factor = jnp.where(
        lane < 2 * span, pltpu.roll(scale, span, 1),
        jnp.where(lane < 3 * span, pltpu.roll(scale, 2 * span, 1), 1.0),
    )
    result = jnp.where(lane < span, best, jnp.sum(every * factor, axis=0, keepdims=True))
    mine = result
    for k in range(1, group):
        mine = jnp.where(section % group == k, pltpu.roll(result, LANES - k * rows, 1), mine)
    top = mine
    total = pltpu.roll(mine, LANES - span, 1)
    moment = pltpu.roll(mine, LANES - 2 * span, 1)
    picked = pltpu.roll(mine, LANES - 3 * span, 1)
    top, total, moment, picked = [item[:, :rows] for item in (top, total, moment, picked)]
    lse = top + jnp.log(total)
    logp = picked - lse
    ent = lse - moment / total
    live = (lane[:, :rows] < len_v[...]).astype(jnp.float32)
    out_logp[...] = logp * live
    out_ent[...] = ent * live
    out_kl[...] = (logp - ref_v[...]) * live
    repeat(peers - 1, lambda k: stat_copy(k).wait_send())


def per_device(sections, tensors, hidden, weight, ids, ref_logp, lengths):
    rows, width = hidden.shape
    depth, voc_dev = weight.shape
    pairs = sections // 2
    peers = sections * tensors
    chunks = sections * rows * 4 // LANES
    anywhere = pl.BlockSpec(memory_space=pltpu.HBM)
    dma = pltpu.SemaphoreType.DMA
    outs = pl.pallas_call(
        functools.partial(kernel, sections, tensors),
        out_shape=[jax.ShapeDtypeStruct((1, rows), jnp.float32)] * 3,
        in_specs=[anywhere] * 5,
        out_specs=[pl.BlockSpec(memory_space=pltpu.VMEM)] * 3,
        scratch_shapes=[
            pltpu.VMEM((tensors, width, voc_dev), jnp.bfloat16),
            pltpu.VMEM((tensors, sections, rows, width), jnp.bfloat16),
            pltpu.VMEM((sections, 1, rows), jnp.int32),
            pltpu.VMEM((1, rows), jnp.float32),
            pltpu.VMEM((1, 1), jnp.int32),
            pltpu.VMEM((chunks, 1, LANES), jnp.float32),
            pltpu.VMEM((peers, 1, LANES), jnp.float32),
            dma((tensors,)),
            dma((4,)),
            dma((tensors, sections)),
            dma((tensors,)),
            dma((tensors, pairs)),
            dma((tensors, pairs)),
            dma((sections,)),
            dma((sections,)),
            dma((peers,)),
            dma((peers,)),
        ],
        compiler_params=pltpu.CompilerParams(
            collective_id=0, has_side_effects=True, vmem_limit_bytes=48 * 1024 * 1024
        ),
    )(hidden, weight, ids.reshape(1, rows), ref_logp.reshape(1, rows), lengths.reshape(1, 1))
    return tuple(item.reshape(rows) for item in outs)


def solution(mesh):
    in_specs = (
        P(("section", "dp"), "tensor"),
        P(None, ("section", "tensor")),
        P(("section", "dp")),
        P(("section", "dp")),
        P(("section", "dp")),
    )
    out_specs = (P(("section", "dp")), P(("section", "dp")), P(("section", "dp")))
    return jax.shard_map(
        functools.partial(per_device, mesh.shape["section"], mesh.shape["tensor"]),
        mesh=mesh, in_specs=in_specs, out_specs=out_specs, check_vma=False,
    )
```

```python
import functools

import jax
import jax.numpy as jnp
from jax import lax
from jax.experimental import pallas as pl
from jax.experimental.pallas import tpu as pltpu
from jax.sharding import PartitionSpec as P

MESH = pl.DeviceIdType.MESH
LANES = 128


def repeat(count, body):
    if count <= 16:
        for i in range(count):
            body(i)
    else:
        lax.fori_loop(0, count, lambda i, _: (body(i), 0)[1], 0)


def kernel(
    sections, tensors, hidden, weight, ids, ref_logp, lengths,
    out,
    w, g, id_rows, ref_v, len_v, stat, merged,
    w_sem, own_sem, block_recv, a_send, b_send, c_send, id_send, id_recv, s_send, s_recv,
):
    rows, width = hidden.shape
    voc_dev = weight.shape[1]
    pairs = sections // 2
    peers = sections * tensors
    group = LANES // (4 * rows)
    section = lax.axis_index("section")
    tensor = lax.axis_index("tensor")
    core = section % 2
    pair = section // 2
    sibling = section + 1 - 2 * core
    me = section * tensors + tensor

    def nth(j):
        if tensors & (tensors - 1):
            return (tensor + j) % tensors, (tensor + tensors - j) % tensors
        at, bit = tensor, 1
        while bit < tensors:
            if j & bit:
                at = at + bit - 2 * bit * ((tensor // bit) % 2)
            bit *= 2
        return at, at

    loads = []
    for j in range(tensors):
        _, source = nth(j)
        begin = pl.multiple_of(source * width, width)
        loads.append(pltpu.make_async_copy(weight.at[pl.ds(begin, width)], w.at[j], w_sem.at[j]))
        loads[-1].start()
    own = pltpu.make_async_copy(hidden, g.at[tensor, section], own_sem.at[0])
    own_id = pltpu.make_async_copy(ids, id_rows.at[section], own_sem.at[1])
    own_ref = pltpu.make_async_copy(ref_logp, ref_v, own_sem.at[2])
    own_len = pltpu.make_async_copy(lengths, len_v, own_sem.at[3])
    for copy in (own, own_id, own_ref, own_len):
        copy.start()

    barrier = pltpu.get_barrier_semaphore()

    def greet(axis, at, size, k):
        pl.semaphore_signal(
            barrier, inc=1, device_id={axis: (at + k + 1) % size}, device_id_type=MESH
        )

    repeat(tensors - 1, lambda k: greet("tensor", tensor, tensors, k))
    repeat(sections - 1, lambda k: greet("section", section, sections, k))
    pl.semaphore_wait(barrier, tensors + sections - 2)

    def block(source, t, s, send, to_section, to_tensor):
        return pltpu.make_async_remote_copy(
            src_ref=source, dst_ref=g.at[t, s], send_sem=send, recv_sem=block_recv.at[t, s],
            device_id={"section": to_section, "tensor": to_tensor}, device_id_type=MESH,
        )

    def copy_a(j):
        return block(hidden, tensor, section, a_send.at[j], section, nth(j)[0])

    def copy_b(j, source, k):
        to = ((pair + k + 1) % pairs) * 2 + core
        return block(source, nth(j)[1], section, b_send.at[j, k], to, tensor)

    def copy_c(j, source, k):
        s = ((pair + k) % pairs) * 2 + core
        return block(source, nth(j)[1], s, c_send.at[j, k], sibling, tensor)

    def arrived(t, s):
        pltpu.make_async_copy(g.at[t, s], g.at[t, s], block_recv.at[t, s]).wait()

    def id_copy(k):
        return pltpu.make_async_remote_copy(
            src_ref=ids, dst_ref=id_rows.at[section], send_sem=id_send.at[k],
            recv_sem=id_recv.at[section],
            device_id={"section": (section + k + 1) % sections}, device_id_type=MESH,
        )

    repeat(pairs - 1, lambda k: copy_b(0, hidden, k).start())
    for j in range(1, tensors):
        copy_a(j).start()
    copy_c(0, hidden, 0).start()
    repeat(sections - 1, lambda k: id_copy(k).start())

    own.wait()

    def forward_own(j):
        t = nth(j)[1]
        arrived(t, section)
        repeat(pairs - 1, lambda k: copy_b(j, g.at[t, section], k).start())
        copy_c(j, g.at[t, section], 0).start()

    def forward_pairs(j):
        t = nth(j)[1]

        def one(k):
            s = ((pair + k + 1) % pairs) * 2 + core
            arrived(t, s)
            copy_c(j, g.at[t, s], k + 1).start()

        repeat(pairs - 1, one)

    def product(j):
        t = nth(j)[1]
        repeat(pairs, lambda k: arrived(t, ((pair + k) % pairs) * 2 + 1 - core))
        loads[j].wait()
        x = g[t].astype(jnp.float32).reshape(sections * rows, width).astype(jnp.bfloat16)
        return jnp.dot(x, w[j], preferred_element_type=jnp.float32)

    forward_own(1)
    forward_pairs(0)
    for j in range(2, tensors):
        forward_own(j)
    logits = product(0)
    forward_pairs(1)
    for j in range(2, tensors):
        forward_pairs(j)
        logits = logits + product(j - 1)
    logits = logits + product(tensors - 1)

    own_id.wait()

    def id_wait(k):
        s = (section + k + 1) % sections
        pltpu.make_async_copy(id_rows.at[s], id_rows.at[s], id_recv.at[s]).wait()

    repeat(sections - 1, id_wait)
    eye = lax.broadcasted_iota(jnp.int32, (rows, rows), 0) == lax.broadcasted_iota(
        jnp.int32, (rows, rows), 1
    )
    columns = []
    for s in range(sections):
        row = jnp.broadcast_to(id_rows[s].astype(jnp.float32), (rows, rows))
        columns.append(jnp.sum(jnp.where(eye, row, 0.0), axis=1, keepdims=True))
    column = jnp.concatenate(columns, axis=0).astype(jnp.int32) - me * voc_dev

    top = jnp.max(logits, axis=1, keepdims=True)
    expo = jnp.exp(logits - top)
    total = jnp.sum(expo, axis=1, keepdims=True)
    moment = jnp.sum(expo * logits, axis=1, keepdims=True)
    at = lax.broadcasted_iota(jnp.int32, logits.shape, 1)
    picked = jnp.sum(jnp.where(at == column, logits, 0.0), axis=1, keepdims=True)

    span = group * rows
    diagonal = lax.broadcasted_iota(jnp.int32, (LANES, LANES), 0) == lax.broadcasted_iota(
        jnp.int32, (LANES, LANES), 1
    )
    for c in range(sections // group):
        piece = jnp.concatenate(
            [item[c * span : (c + 1) * span] for item in (top, total, moment, picked)], axis=0
        )
        stat[c] = jnp.sum(
            jnp.where(diagonal, jnp.broadcast_to(piece, (LANES, LANES)), 0.0), axis=0, keepdims=True
        )

    def stat_copy(k):
        other = (me + k + 1) % peers
        to = other // tensors
        return pltpu.make_async_remote_copy(
            src_ref=stat.at[to // group], dst_ref=merged.at[me], send_sem=s_send.at[k],
            recv_sem=s_recv.at[me],
            device_id={"section": to, "tensor": other % tensors}, device_id_type=MESH,
        )

    repeat(peers - 1, lambda k: stat_copy(k).start())
    merged[me] = stat[section // group]

    for j in range(1, tensors):
        copy_a(j).wait_send()
    for j in range(tensors):
        repeat(pairs - 1, lambda k: copy_b(j, hidden, k).wait_send())
        repeat(pairs, lambda k: copy_c(j, hidden, k).wait_send())
    repeat(sections - 1, lambda k: id_copy(k).wait_send())
    own_ref.wait()
    own_len.wait()

    def stat_wait(k):
        other = (me + k + 1) % peers
        pltpu.make_async_copy(merged.at[other], merged.at[other], s_recv.at[other]).wait()

    repeat(peers - 1, stat_wait)
    every = merged[...].reshape(peers, LANES)
    lane = lax.broadcasted_iota(jnp.int32, (1, LANES), 1)
    best = jnp.max(every, axis=0, keepdims=True)
    scale = jnp.exp(every - best)
    factor = jnp.where(
        lane < 2 * span, pltpu.roll(scale, span, 1),
        jnp.where(lane < 3 * span, pltpu.roll(scale, 2 * span, 1), 1.0),
    )
    result = jnp.where(lane < span, best, jnp.sum(every * factor, axis=0, keepdims=True))
    mine = result
    for k in range(1, group):
        mine = jnp.where(section % group == k, pltpu.roll(result, LANES - k * rows, 1), mine)
    top = mine
    total = pltpu.roll(mine, LANES - span, 1)
    moment = pltpu.roll(mine, LANES - 2 * span, 1)
    picked = pltpu.roll(mine, LANES - 3 * span, 1)
    top, total, moment, picked = [item[:, :rows] for item in (top, total, moment, picked)]
    lse = top + jnp.log(total)
    logp = picked - lse
    ent = lse - moment / total
    live = (lane[:, :rows] < len_v[...]).astype(jnp.float32)
    out[...] = jnp.concatenate([logp * live, ent * live, (logp - ref_v[...]) * live], axis=0)
    repeat(peers - 1, lambda k: stat_copy(k).wait_send())


def per_device(sections, tensors, hidden, weight, ids, ref_logp, lengths):
    rows, width = hidden.shape
    depth, voc_dev = weight.shape
    pairs = sections // 2
    peers = sections * tensors
    chunks = sections * rows * 4 // LANES
    anywhere = pl.BlockSpec(memory_space=pltpu.HBM)
    dma = pltpu.SemaphoreType.DMA
    outs = pl.pallas_call(
        functools.partial(kernel, sections, tensors),
        out_shape=jax.ShapeDtypeStruct((3, rows), jnp.float32),
        in_specs=[anywhere] * 5,
        out_specs=pl.BlockSpec(memory_space=pltpu.VMEM),
        scratch_shapes=[
            pltpu.VMEM((tensors, width, voc_dev), jnp.bfloat16),
            pltpu.VMEM((tensors, sections, rows, width), jnp.bfloat16),
            pltpu.VMEM((sections, 1, rows), jnp.int32),
            pltpu.VMEM((1, rows), jnp.float32),
            pltpu.VMEM((1, 1), jnp.int32),
            pltpu.VMEM((chunks, 1, LANES), jnp.float32),
            pltpu.VMEM((peers, 1, LANES), jnp.float32),
            dma((tensors,)),
            dma((4,)),
            dma((tensors, sections)),
            dma((tensors,)),
            dma((tensors, pairs)),
            dma((tensors, pairs)),
            dma((sections,)),
            dma((sections,)),
            dma((peers,)),
            dma((peers,)),
        ],
        compiler_params=pltpu.CompilerParams(
            collective_id=0, has_side_effects=True, vmem_limit_bytes=63 * 1024 * 1024
        ),
    )(hidden, weight, ids.reshape(1, rows), ref_logp.reshape(1, rows), lengths.reshape(1, 1))
    return outs[0], outs[1], outs[2]


def solution(mesh):
    in_specs = (
        P(("section", "dp"), "tensor"),
        P(None, ("section", "tensor")),
        P(("section", "dp")),
        P(("section", "dp")),
        P(("section", "dp")),
    )
    out_specs = (P(("section", "dp")), P(("section", "dp")), P(("section", "dp")))
    return jax.shard_map(
        functools.partial(per_device, mesh.shape["section"], mesh.shape["tensor"]),
        mesh=mesh, in_specs=in_specs, out_specs=out_specs, check_vma=False,
    )
```
